32 devices in a mesh: row: 4 (over y, x), col: 8 (over z, core).
Axes of the slice: x: 2, y: 2, z: 4, core: 2. Of those that a mesh axis runs over, the one named last changes fastest.
Arguments:
- features: float32 [16384, 256], P(('col', 'row')), may hold values from -6 to 6
- weight: float32 [256, 256], replicated, may hold values from -0.375 to 0.375
- cotangent: float32 [16384, 256], P(('row', 'col')), may hold values from -6 to 6
- tile_values: float32 [4, 8, 128, 128, 128], P('row', 'col'), as said below
- tile_rows: int32 [4, 8, 128], P('row', 'col'), may hold values from 0 to 31
- tile_cols: int32 [4, 8, 128], P('row', 'col'), may hold values from 0 to 15
- tile_count: int32 [4, 8], P('row', 'col'), may hold values from 16 to 128, as said below
Outputs:
- output: float32 [16384, 256], P(('row', 'col'))
- feature_grad: float32 [16384, 256], P(('col', 'row'))
- weight_grad: float32 [256, 256], replicated
The draws below stay inside these ranges and needn't reach their ends.
Inputs may be any that keep to these rules, and one draw needn't show every extreme that they name: `tile_count`: the number of live slots of a grid cell is 128, 64, 32 or 16; some cell has 128. `tile_values`: entries are zero or positive.
All inputs are finite; a program needn't handle non-finite values.
Results may differ from the reference program's by a relative error of at most 0.0001.
Values sent between devices are 32-bit elements; how exact they have to be, the bound alone decides.
A program may use at most 128 MiB of HBM per device.

```python
import math
import jax
import jax.numpy as jnp
from jax import lax

F = 256
BLK = 128
ROWS_DEV = 512
TILES_DEV = 128
NODES = 16384
RBLK = 32
CBLK = 16
N_ROW = 4
N_COL = 8


def draw_tile_values(key, part):
    first_key, second_key = jax.random.split(jax.random.fold_in(key, 11))
    shape = (N_ROW, N_COL, TILES_DEV, BLK, BLK)
    columns_per_row = TILES_DEV * BLK * BLK / ROWS_DEV
    density = min(0.5, 50.0 / columns_per_row)
    degree = columns_per_row * density * 0.5
    factor = 1.0 / degree
    magnitude = jax.random.uniform(first_key, shape, jnp.float32, 0.3, 1.7) * factor
    present = jax.random.uniform(second_key, shape, jnp.float32) < density
    return jnp.where(present, magnitude, jnp.zeros(shape, jnp.float32))


def draw_tile_count(key, part):
    shift_key, pick_key = jax.random.split(jax.random.fold_in(key, 23))
    shifts = jax.random.randint(shift_key, (N_ROW * N_COL,), 0, 4, dtype=jnp.int32)
    counts = jnp.right_shift(jnp.full((N_ROW * N_COL,), TILES_DEV, jnp.int32), shifts)
    chosen = jax.random.randint(pick_key, (), 0, N_ROW * N_COL, dtype=jnp.int32)
    counts = counts.at[chosen].set(TILES_DEV)
    return counts.reshape(N_ROW, N_COL)


def plant(entries, stream_key, smallest, top_value):
    longest = entries.shape.index(max(entries.shape))
    spots = []
    for shift in (0, 1):
        where = [jax.random.randint(jax.random.fold_in(stream_key, axis), (), 0, length) for axis, length in enumerate(entries.shape)]
        where[longest] = (where[longest] + shift) % entries.shape[longest]
        spots.append(tuple(where))
    return entries.at[spots[0]].set(smallest).at[spots[1]].set(top_value)


def levels(key, dims, pieces, least, high):
    def one(position, shards_of):
        draws = jax.random.uniform(jax.random.fold_in(jax.random.fold_in(key, 6), position), (shards_of,), jnp.float32, least / len(pieces), high / len(pieces))
        return jnp.repeat(jnp.exp(draws), dims[position] // shards_of).reshape((-1,) + (1,) * (len(dims) - position - 1))

    level = one(*pieces[0])
    for cut in pieces[1:]:
        level = level * one(*cut)
    return level


def centred(key, dims, scale, limit, cuts=(), held_as=jnp.bfloat16):
    loudness = levels(key, dims, cuts, -0.22, 0.18) if cuts else 1.0
    values = jax.random.normal(key, dims, jnp.float32) * scale * loudness
    return jnp.minimum(jnp.maximum(values, -limit), limit).astype(held_as)


def setup_inputs(seed: int = 0) -> dict:
    arg_keys = jax.random.split(jax.random.key(seed), 8)
    features = centred(arg_keys[0], (NODES, F), 1.0, 6.0, ((0, 32),), jnp.float32)
    weight = centred(arg_keys[1], (F, F), F ** -0.5, 0.375, (), jnp.float32)
    cotangent = centred(arg_keys[2], (NODES, F), 1.0, 6.0, ((0, 32),), jnp.float32)
    tile_values = draw_tile_values(jax.random.fold_in(arg_keys[7], 71), 0)
    tile_rows = plant(jax.random.randint(arg_keys[4], (N_ROW, N_COL, TILES_DEV), 0, RBLK), jax.random.fold_in(arg_keys[4], 1), 0, RBLK - 1).astype(jnp.int32)
    tile_cols = plant(jax.random.randint(arg_keys[5], (N_ROW, N_COL, TILES_DEV), 0, CBLK), jax.random.fold_in(arg_keys[5], 1), 0, CBLK - 1).astype(jnp.int32)
    tile_count = draw_tile_count(jax.random.fold_in(arg_keys[7], 71), 0)
    return {"features": features, "weight": weight, "cotangent": cotangent, "tile_values": tile_values, "tile_rows": tile_rows, "tile_cols": tile_cols, "tile_count": tile_count}


def combine_tiles(tiles, row_ids, col_ids, count, source, out_blocks, transpose):
    highest = lax.Precision.HIGHEST
    blocks_in = source.reshape(-1, BLK, F)
    if transpose:
        picked = blocks_in[row_ids]
        product = jnp.einsum('tji,tjf->tif', tiles, picked, precision=highest)
        put_ids = col_ids
    else:
        picked = blocks_in[col_ids]
        product = jnp.einsum('tij,tjf->tif', tiles, picked, precision=highest)
        put_ids = row_ids
    alive_mask = (jnp.arange(TILES_DEV, dtype=jnp.int32) < count).astype(jnp.float32)
    product = product * alive_mask[:, None, None]
    summed = jax.ops.segment_sum(product, put_ids, num_segments=out_blocks)
    return summed.reshape(out_blocks * BLK, F)

def reference(features, weight, cotangent, tile_values, tile_rows, tile_cols, tile_count):
    highest = lax.Precision.HIGHEST
    row_group = NODES // N_ROW
    col_group = NODES // N_COL
    projected = jnp.dot(features, weight, precision=highest)
    pre = jnp.zeros((NODES, F), jnp.float32)
    for r in range(N_ROW):
        for c in range(N_COL):
            term = combine_tiles(tile_values[r, c], tile_rows[r, c], tile_cols[r, c], tile_count[r, c], projected[c * col_group:(c + 1) * col_group], row_group // BLK, False)
            pre = pre.at[r * row_group:(r + 1) * row_group].add(term)
    sigma = jax.nn.sigmoid(pre)
    output = pre * sigma
    grad_pre = cotangent * sigma * (1.0 + pre * (1.0 - sigma))
    grad_projected = jnp.zeros((NODES, F), jnp.float32)
    for r in range(N_ROW):
        for c in range(N_COL):
            term = combine_tiles(tile_values[r, c], tile_rows[r, c], tile_cols[r, c], tile_count[r, c], grad_pre[r * row_group:(r + 1) * row_group], col_group // BLK, True)
            grad_projected = grad_projected.at[c * col_group:(c + 1) * col_group].add(term)
    feature_grad = jnp.dot(grad_projected, weight.T, precision=highest)
    weight_grad = jnp.dot(features.T, grad_projected, precision=highest) / math.sqrt(NODES)
    return (output, feature_grad, weight_grad)
```

```python
import functools
import math

import jax
import jax.numpy as jnp
from jax import lax
from jax.experimental import pallas as pl
from jax.experimental.pallas import tpu as pltpu
from jax.sharding import PartitionSpec as P

F32 = jnp.float32
BF16 = jnp.bfloat16
MESH = pl.DeviceIdType.MESH
VMEM_LIMIT = 60 * 1024 * 1024
HIGHEST = lax.Precision.HIGHEST


def split(x):
    hi = x.astype(BF16)
    return hi, (x - hi.astype(F32)).astype(BF16)


def params(collective_id=None):
    if collective_id is None:
        return pltpu.CompilerParams(vmem_limit_bytes=VMEM_LIMIT)
    return pltpu.CompilerParams(
        vmem_limit_bytes=VMEM_LIMIT, collective_id=collective_id, has_side_effects=True
    )


def tile_kernel(group, transpose, fetch_ref, put_ref, count_ref, tiles_ref, source_ref, out_ref, hi_ref, lo_ref):
    step = pl.program_id(0)
    edge = tiles_ref.shape[1]

    @pl.when(step == 0)
    def _():
        out_ref[...] = jnp.zeros_like(out_ref)

        @pl.loop(0, source_ref.shape[0] // edge)
        def _(b):
            rows = pl.ds(pl.multiple_of(b * edge, edge), edge)
            hi, lo = split(source_ref[rows, :])
            hi_ref[rows, :] = hi
            lo_ref[rows, :] = lo

    @pl.when(step * group < count_ref[0])
    def _():
        for t in range(group):
            slot = step * group + t
            fetch = pl.ds(pl.multiple_of(fetch_ref[slot] * edge, edge), edge)
            put = pl.ds(pl.multiple_of(put_ref[slot] * edge, edge), edge)
            tile = tiles_ref[t]
            if transpose:
                tile = tile.T
            a_hi, a_lo = split(tile)
            b_hi, b_lo = hi_ref[fetch, :], lo_ref[fetch, :]
            product = jnp.dot(
                jnp.concatenate([a_hi, a_lo], axis=1),
                jnp.concatenate([b_hi, b_hi], axis=0),
                preferred_element_type=F32,
            ) + jnp.dot(a_hi, b_lo, preferred_element_type=F32)
            out_ref[put, :] += product


def combine_tiles(tiles, fetch_ids, put_ids, count, source, out_rows, transpose):
    slots, edge, _ = tiles.shape
    width = source.shape[1]
    group = math.gcd(16, slots)

    def tile_index(i, fetch, put, n):
        return (jnp.minimum(i, (n[0] - 1) // group), 0, 0)

    return pl.pallas_call(
        functools.partial(tile_kernel, group, transpose),
        grid_spec=pltpu.PrefetchScalarGridSpec(
            num_scalar_prefetch=3,
            grid=(slots // group,),
            in_specs=[
                pl.BlockSpec((group, edge, edge), tile_index),
                pl.BlockSpec(source.shape, lambda i, *_: (0, 0), pipeline_mode=pl.Buffered(1)),
            ],
            out_specs=pl.BlockSpec((out_rows, width), lambda i, *_: (0, 0), pipeline_mode=pl.Buffered(1)),
            scratch_shapes=[pltpu.VMEM(source.shape, BF16), pltpu.VMEM(source.shape, BF16)],
        ),
        out_shape=jax.ShapeDtypeStruct((out_rows, width), F32),
        compiler_params=params(),
    )(fetch_ids, put_ids, count, tiles, source)


def gather_kernel(n, x_ref, out_ref, send_sem, recv_sem, own_sem):
    me = lax.axis_index("row")
    rows = x_ref.shape[0]
    barrier = pltpu.get_barrier_semaphore()
    for j in range(1, n):
        pl.semaphore_signal(barrier, inc=1, device_id={"row": lax.rem(me + j, n)}, device_id_type=MESH)
    pl.semaphore_wait(barrier, n - 1)

    def copy(j, block):
        return pltpu.make_async_remote_copy(
            src_ref=x_ref,
            dst_ref=out_ref.at[pl.ds(pl.multiple_of(block * rows, rows), rows), :],
            send_sem=send_sem.at[j],
            recv_sem=recv_sem.at[j],
            device_id={"row": lax.rem(me + j, n)},
            device_id_type=MESH,
        )

    for j in range(1, n):
        copy(j, me).start()
    own = pltpu.make_async_copy(x_ref, out_ref.at[pl.ds(pl.multiple_of(me * rows, rows), rows), :], own_sem)
    own.start()
    own.wait()
    for j in range(1, n):
        copy(j, me).wait_send()
        copy(j, lax.rem(me + n - j, n)).wait_recv()


def gather_rows(x, n):
    return pl.pallas_call(
        functools.partial(gather_kernel, n),
        in_specs=[pl.BlockSpec(memory_space=pl.ANY)],
        out_specs=pl.BlockSpec(memory_space=pl.ANY),
        out_shape=jax.ShapeDtypeStruct((n * x.shape[0], x.shape[1]), F32),
        scratch_shapes=[
            pltpu.SemaphoreType.DMA((n,)),
            pltpu.SemaphoreType.DMA((n,)),
            pltpu.SemaphoreType.DMA,
        ],
        compiler_params=params(0),
    )(x)


def middle_kernel(
    zs, chunks,
    part_ref, weight_ref, cot_ref,
    out_ref, grads_ref, term_ref,
    acc, mate, from_left, from_right, grad,
    own_sem, mate_send, mate_recv, right_send, right_recv, left_send, left_recv,
    on_send, back_send, line_recv, share_send, share_recv, keep_sem,
):
    col = lax.axis_index("col")
    z, k = lax.div(col, 2), lax.rem(col, 2)
    rows = cot_ref.shape[0]
    size = rows // chunks
    pair = {"col": z * 2 + (1 - k)}
    right, left = {"col": jnp.minimum(z + 1, zs - 1) * 2 + k}, {"col": jnp.maximum(z - 1, 0) * 2 + k}
    has_left, has_right = z > 0, z < zs - 1

    barrier = pltpu.get_barrier_semaphore()
    pl.semaphore_signal(barrier, inc=1, device_id=pair, device_id_type=MESH)

    @pl.when(has_left)
    def _():
        pl.semaphore_signal(barrier, inc=1, device_id=left, device_id_type=MESH)

    @pl.when(has_right)
    def _():
        pl.semaphore_signal(barrier, inc=1, device_id=right, device_id_type=MESH)

    pl.semaphore_wait(barrier, 1 + has_left.astype(jnp.int32) + has_right.astype(jnp.int32))

    def span(c):
        return pl.ds(pl.multiple_of(c * size, size), size)

    def place(owner, core, c):
        return pl.ds(pl.multiple_of((owner * 2 + core) * rows + c * size, size), size)

    def remote(src, dst, send, recv, device):
        return pltpu.make_async_remote_copy(
            src_ref=src, dst_ref=dst, send_sem=send, recv_sem=recv, device_id=device, device_id_type=MESH
        )

    def own_copy(d):
        block = part_ref.at[pl.ds(pl.multiple_of((d * 2 + k) * rows, rows), rows), :]
        return pltpu.make_async_copy(block, acc.at[d], own_sem.at[d])

    def mate_copy(d, c):
        return remote(
            part_ref.at[place(d, 1 - k, c), :], mate.at[d, span(c)], mate_send.at[d, c], mate_recv.at[d, c], pair
        )

    def to_right(d, c):
        return remote(acc.at[d, span(c)], from_left.at[d, span(c)], right_send.at[d, c], right_recv.at[d, c], right)

    def to_left(d, c):
        return remote(acc.at[d, span(c)], from_right.at[d, span(c)], left_send.at[d, c], left_recv.at[d, c], left)

    def own_on(c):
        return remote(grad.at[span(c)], grads_ref.at[place(z, k, c), :], on_send.at[z, c], line_recv.at[z, c], right)

    def own_back(c):
        return remote(grad.at[span(c)], grads_ref.at[place(z, k, c), :], back_send.at[c], line_recv.at[z, c], left)

    def own_share(c):
        return remote(grad.at[span(c)], grads_ref.at[place(z, k, c), :], share_send.at[z, c], share_recv.at[z, c], pair)

    def own_keep(c):
        return pltpu.make_async_copy(grad.at[span(c)], grads_ref.at[place(z, k, c), :], keep_sem.at[c])

    def pass_on(s, c, device):
        where = grads_ref.at[place(s, k, c), :]
        return remote(where, where, on_send.at[s, c], line_recv.at[s, c], device)

    def share(s, core, c):
        where = grads_ref.at[place(s, core, c), :]
        return remote(where, where, share_send.at[s, c], share_recv.at[s, c], pair)

    @pl.loop(0, zs)
    def _(d):
        own_copy(d).start()

    @pl.loop(0, chunks)
    def _(c):
        @pl.loop(0, zs)
        def _(d):
            mate_copy(d, c).start()

    @pl.loop(0, zs)
    def _(d):
        own_copy(d).wait()

    def add_mate(d, c):
        mate_copy(d, c).wait_recv()
        acc[d, span(c)] += mate[d, span(c)]

    def reduce_chunk(c):
        @pl.loop(0, zs - 1)
        def _(i):
            far = zs - 1 - i

            @pl.when(far > z)
            def _():
                add_mate(far, c)

                @pl.when(has_left)
                def _():
                    to_right(far, c).wait_recv()
                    acc[far, span(c)] += from_left[far, span(c)]

                to_right(far, c).start()

            @pl.when(i < z)
            def _():
                add_mate(i, c)

                @pl.when(has_right)
                def _():
                    to_left(i, c).wait_recv()
                    acc[i, span(c)] += from_right[i, span(c)]

                to_left(i, c).start()

    def finish_chunk(c):
        add_mate(z, c)

        @pl.when(has_left)
        def _():
            to_right(z, c).wait_recv()
            acc[z, span(c)] += from_left[z, span(c)]

        @pl.when(has_right)
        def _():
            to_left(z, c).wait_recv()
            acc[z, span(c)] += from_right[z, span(c)]

        summed = acc[z, span(c)]
        weight = weight_ref[...]
        pre = jnp.dot(summed, weight, precision=HIGHEST, preferred_element_type=F32)
        sigma = jax.nn.sigmoid(pre)
        out_ref[span(c), :] = pre * sigma
        grad_pre = cot_ref[span(c), :] * sigma * (1.0 + pre * (1.0 - sigma))
        grad[span(c)] = lax.dot_general(
            grad_pre, weight, (((1,), (1,)), ((), ())), precision=HIGHEST, preferred_element_type=F32
        )

        @pl.when(has_right)
        def _():
            own_on(c).start()

        @pl.when(has_left)
        def _():
            own_back(c).start()

        own_share(c).start()
        own_keep(c).start()
        term_ref[...] += lax.dot_general(
            summed, grad_pre, (((0,), (0,)), ((), ())), precision=HIGHEST, preferred_element_type=F32
        )

    def relay_chunk(c):
        @pl.loop(1, zs)
        def _(i):
            low, high = z - i, z + i

            @pl.when(low >= 0)
            def _():
                pass_on(low, c, right).wait_recv()

                @pl.when(has_right)
                def _():
                    pass_on(low, c, right).start()

                share(low, k, c).start()

            @pl.when(high < zs)
            def _():
                pass_on(high, c, left).wait_recv()

                @pl.when(has_left)
                def _():
                    pass_on(high, c, left).start()

                share(high, k, c).start()

    term_ref[...] = jnp.zeros_like(term_ref)

    @pl.loop(0, chunks + 2)
    def _(s):
        @pl.when(s < chunks)
        def _():
            reduce_chunk(s)

        @pl.when((s >= 1) & (s <= chunks))
        def _():
            finish_chunk(s - 1)

        @pl.when(s >= 2)
        def _():
            relay_chunk(s - 2)

    @pl.loop(0, chunks)
    def _(c):
        own_share(c).wait_send()
        own_keep(c).wait()

        @pl.when(has_right)
        def _():
            own_on(c).wait_send()

        @pl.when(has_left)
        def _():
            own_back(c).wait_send()

        @pl.loop(0, zs)
        def _(d):
            mate_copy(d, c).wait_send()
            share(d, 1 - k, c).wait_recv()

            @pl.when(d > z)
            def _():
                to_right(d, c).wait_send()
                share(d, k, c).wait_send()

                @pl.when(has_left)
                def _():
                    pass_on(d, c, left).wait_send()

            @pl.when(d < z)
            def _():
                to_left(d, c).wait_send()
                share(d, k, c).wait_send()

                @pl.when(has_right)
                def _():
                    pass_on(d, c, right).wait_send()


def middle(part, weight, cotangent, n_col):
    rows, width = cotangent.shape
    zs, chunks = n_col // 2, 4
    grid2 = pltpu.SemaphoreType.DMA((zs, chunks))
    vmem = pl.BlockSpec(memory_space=pltpu.VMEM)
    blocks = pltpu.VMEM((zs, rows, width), F32)
    return pl.pallas_call(
        functools.partial(middle_kernel, zs, chunks),
        in_specs=[pl.BlockSpec(memory_space=pl.ANY), vmem, vmem],
        out_specs=(vmem, pl.BlockSpec(memory_space=pl.ANY), vmem),
        out_shape=(
            jax.ShapeDtypeStruct((rows, width), F32),
            jax.ShapeDtypeStruct((n_col * rows, width), F32),
            jax.ShapeDtypeStruct((width, width), F32),
        ),
        scratch_shapes=[
            blocks, blocks, blocks, blocks, pltpu.VMEM((rows, width), F32),
            pltpu.SemaphoreType.DMA((zs,)), grid2, grid2, grid2, grid2, grid2, grid2,
            grid2, pltpu.SemaphoreType.DMA((chunks,)), grid2, grid2, grid2, pltpu.SemaphoreType.DMA((chunks,)),
        ],
        compiler_params=params(1),
    )(part, weight, cotangent)


def last_kernel(
    n_row, n_col, scale,
    part_ref, term_ref,
    out_ref, total_ref,
    arrived, first, second,
    own_sem, send_sem, recv_sem, send1, recv1, send2, recv2, send3, recv3,
):
    row, col = lax.axis_index("row"), lax.axis_index("col")
    rows = out_ref.shape[0]
    piece = term_ref.shape[0] // n_col
    barrier = pltpu.get_barrier_semaphore()
    for j in range(1, n_row):
        pl.semaphore_signal(barrier, inc=1, device_id={"row": lax.rem(row + j, n_row)}, device_id_type=MESH)
    for j in range(1, n_col):
        pl.semaphore_signal(barrier, inc=1, device_id={"col": lax.rem(col + j, n_col)}, device_id_type=MESH)
    pl.semaphore_wait(barrier, n_row + n_col - 2)

    def block(i):
        return part_ref.at[pl.ds(pl.multiple_of(i * rows, rows), rows), :]

    def rows_of(i):
        return pl.ds(pl.multiple_of(i * piece, piece), piece)

    def bulk(j):
        to = lax.rem(row + j, n_row)
        return pltpu.make_async_remote_copy(
            src_ref=block(to), dst_ref=arrived.at[j], send_sem=send_sem.at[j], recv_sem=recv_sem.at[j],
            device_id={"row": to}, device_id_type=MESH,
        )

    def scatter(j):
        to = lax.rem(col + j, n_col)
        return pltpu.make_async_remote_copy(
            src_ref=term_ref.at[rows_of(to), :], dst_ref=first.at[j], send_sem=send1.at[j], recv_sem=recv1.at[j],
            device_id={"col": to}, device_id_type=MESH,
        )

    def exchange(j, slot):
        return pltpu.make_async_remote_copy(
            src_ref=first.at[0], dst_ref=second.at[slot], send_sem=send2.at[j], recv_sem=recv2.at[j],
            device_id={"row": lax.rem(row + j, n_row)}, device_id_type=MESH,
        )

    def spread(j, owner):
        where = total_ref.at[rows_of(owner), :]
        return pltpu.make_async_remote_copy(
            src_ref=where, dst_ref=where, send_sem=send3.at[j], recv_sem=recv3.at[j],
            device_id={"col": lax.rem(col + j, n_col)}, device_id_type=MESH,
        )

    own = pltpu.make_async_copy(block(row), arrived.at[0], own_sem)
    own.start()
    for j in range(1, n_col):
        scatter(j).start()
    bulk(1).start()
    first[0] = term_ref[rows_of(col), :]
    for j in range(1, n_col):
        scatter(j).wait_recv()
        first[0] += first[j]
    for j in range(1, n_row):
        exchange(j, row).start()
    for j in range(2, n_row):
        bulk(j).start()
    second[row] = first[0]
    for j in range(1, n_row):
        exchange(j, lax.rem(row + n_row - j, n_row)).wait_recv()
    summed = second[0]
    for i in range(1, n_row):
        summed += second[i]
    total_ref[rows_of(col), :] = summed * scale
    for j in range(1, n_col):
        spread(j, col).start()
    own.wait()
    for j in range(1, n_row):
        bulk(j).wait_recv()
    out_ref[...] = arrived[0]
    for j in range(1, n_row):
        out_ref[...] += arrived[j]
    for j in range(1, n_row):
        bulk(j).wait_send()
        exchange(j, row).wait_send()
    for j in range(1, n_col):
        scatter(j).wait_send()
        spread(j, col).wait_send()
        spread(j, lax.rem(col + n_col - j, n_col)).wait_recv()


def last(part, term, n_row, n_col, scale):
    rows, width = part.shape[0] // n_row, part.shape[1]
    piece = term.shape[0] // n_col
    vmem = pl.BlockSpec(memory_space=pltpu.VMEM)
    by_row, by_col = pltpu.SemaphoreType.DMA((n_row,)), pltpu.SemaphoreType.DMA((n_col,))
    return pl.pallas_call(
        functools.partial(last_kernel, n_row, n_col, scale),
        in_specs=[pl.BlockSpec(memory_space=pl.ANY), vmem],
        out_specs=(vmem, vmem),
        out_shape=(jax.ShapeDtypeStruct((rows, width), F32), jax.ShapeDtypeStruct(term.shape, F32)),
        scratch_shapes=[
            pltpu.VMEM((n_row, rows, width), F32),
            pltpu.VMEM((n_col, piece, width), F32),
            pltpu.VMEM((n_row, piece, width), F32),
            pltpu.SemaphoreType.DMA, by_row, by_row, by_col, by_col, by_row, by_row, by_col, by_col,
        ],
        compiler_params=params(2),
    )(part, term)


def local(n_row, n_col, features, weight, cotangent, tile_values, tile_rows, tile_cols, tile_count):
    tiles, row_ids, col_ids = tile_values[0, 0], tile_rows[0, 0], tile_cols[0, 0]
    count = tile_count.reshape(1)
    rows = features.shape[0]
    gathered = gather_rows(features, n_row)
    part = combine_tiles(tiles, col_ids, row_ids, count, gathered, rows * n_col, False)
    output, grads, term = middle(part, weight, cotangent, n_col)
    part_grad = combine_tiles(tiles, row_ids, col_ids, count, grads, rows * n_row, True)
    scale = 1.0 / math.sqrt(rows * n_row * n_col)
    returned, weight_grad = last(part_grad, term, n_row, n_col, scale)
    return (output, returned, weight_grad)


def solution(mesh):
    placed = (
        P(("col", "row"), None),
        P(),
        P(("row", "col"), None),
        P("row", "col", None, None, None),
        P("row", "col", None),
        P("row", "col", None),
        P("row", "col"),
    )
    return jax.shard_map(
        functools.partial(local, mesh.shape["row"], mesh.shape["col"]),
        mesh=mesh,
        in_specs=placed,
        out_specs=(P(("row", "col"), None), P(("col", "row"), None), P()),
        check_vma=False,
    )
```

```python
import functools
import math

import jax
import jax.numpy as jnp
from jax import lax
from jax.experimental import pallas as pl
from jax.experimental.pallas import tpu as pltpu
from jax.sharding import PartitionSpec as P

F32 = jnp.float32
BF16 = jnp.bfloat16
MESH = pl.DeviceIdType.MESH
VMEM_LIMIT = 60 * 1024 * 1024
DENSE = True
HIGHEST = lax.Precision.HIGHEST


def split(x):
    hi = x.astype(BF16)
    return hi, (x - hi.astype(F32)).astype(BF16)


def dot3(a, b_hi, b_lo):
    a_hi, a_lo = split(a)
    dot = functools.partial(jnp.dot, preferred_element_type=F32)
    return dot(a_hi, b_hi) + (dot(a_lo, b_hi) + dot(a_hi, b_lo))


def params(collective_id=None):
    if collective_id is None:
        return pltpu.CompilerParams(vmem_limit_bytes=VMEM_LIMIT)
    return pltpu.CompilerParams(
        vmem_limit_bytes=VMEM_LIMIT, collective_id=collective_id, has_side_effects=True
    )


def tile_kernel(group, transpose, fetch_ref, put_ref, count_ref, tiles_ref, source_ref, out_ref, hi_ref, lo_ref):
    step = pl.program_id(0)
    edge = tiles_ref.shape[1]

    @pl.when(step == 0)
    def _():
        out_ref[...] = jnp.zeros_like(out_ref)

        @pl.loop(0, source_ref.shape[0] // edge)
        def _(b):
            rows = pl.ds(pl.multiple_of(b * edge, edge), edge)
            hi, lo = split(source_ref[rows, :])
            hi_ref[rows, :] = hi
            lo_ref[rows, :] = lo

    @pl.when(step * group < count_ref[0])
    def _():
        for t in range(group):
            slot = step * group + t
            fetch = pl.ds(pl.multiple_of(fetch_ref[slot] * edge, edge), edge)
            put = pl.ds(pl.multiple_of(put_ref[slot] * edge, edge), edge)
            tile = tiles_ref[t]
            if transpose:
                tile = tile.T
            a_hi, a_lo = split(tile)
            b_hi, b_lo = hi_ref[fetch, :], lo_ref[fetch, :]
            product = jnp.dot(
                jnp.concatenate([a_hi, a_lo], axis=1),
                jnp.concatenate([b_hi, b_hi], axis=0),
                preferred_element_type=F32,
            ) + jnp.dot(a_hi, b_lo, preferred_element_type=F32)
            out_ref[put, :] += product


def combine_tiles(tiles, fetch_ids, put_ids, count, source, out_rows, transpose):
    slots, edge, _ = tiles.shape
    width = source.shape[1]
    group = math.gcd(16, slots)

    def tile_index(i, fetch, put, n):
        return (jnp.minimum(i, (n[0] - 1) // group), 0, 0)

    return pl.pallas_call(
        functools.partial(tile_kernel, group, transpose),
        grid_spec=pltpu.PrefetchScalarGridSpec(
            num_scalar_prefetch=3,
            grid=(slots // group,),
            in_specs=[
                pl.BlockSpec((group, edge, edge), tile_index),
                pl.BlockSpec(source.shape, lambda i, *_: (0, 0), pipeline_mode=pl.Buffered(1)),
            ],
            out_specs=pl.BlockSpec((out_rows, width), lambda i, *_: (0, 0), pipeline_mode=pl.Buffered(1)),
            scratch_shapes=[pltpu.VMEM(source.shape, BF16), pltpu.VMEM(source.shape, BF16)],
        ),
        out_shape=jax.ShapeDtypeStruct((out_rows, width), F32),
        compiler_params=params(),
    )(fetch_ids, put_ids, count, tiles, source)


def gather_kernel(n, x_ref, out_ref, send_sem, recv_sem, own_sem):
    me = lax.axis_index("row")
    rows = x_ref.shape[0]
    barrier = pltpu.get_barrier_semaphore()
    for j in range(1, n):
        pl.semaphore_signal(barrier, inc=1, device_id={"row": lax.rem(me + j, n)}, device_id_type=MESH)
    pl.semaphore_wait(barrier, n - 1)

    def copy(j, block):
        return pltpu.make_async_remote_copy(
            src_ref=x_ref,
            dst_ref=out_ref.at[pl.ds(pl.multiple_of(block * rows, rows), rows), :],
            send_sem=send_sem.at[j],
            recv_sem=recv_sem.at[j],
            device_id={"row": lax.rem(me + j, n)},
            device_id_type=MESH,
        )

    for j in range(1, n):
        copy(j, me).start()
    own = pltpu.make_async_copy(x_ref, out_ref.at[pl.ds(pl.multiple_of(me * rows, rows), rows), :], own_sem)
    own.start()
    own.wait()
    for j in range(1, n):
        copy(j, me).wait_send()
        copy(j, lax.rem(me + n - j, n)).wait_recv()


def gather_square_kernel(parts, x_ref, out_ref, send_sem, recv_sem, own_sem):
    me = lax.axis_index("row")
    rows = x_ref.shape[0]
    size = rows // parts
    x_bit, y_bit = lax.rem(me, 2), lax.div(me, 2)
    by_x, by_y = y_bit * 2 + (1 - x_bit), (1 - y_bit) * 2 + x_bit
    corner = 3 - me
    barrier = pltpu.get_barrier_semaphore()
    for peer in (by_x, by_y):
        pl.semaphore_signal(barrier, inc=1, device_id={"row": peer}, device_id_type=MESH)
    pl.semaphore_wait(barrier, 2)

    def at(owner, q):
        return out_ref.at[pl.ds(pl.multiple_of(owner * rows + q * size, size), size), :]

    def copy(source, owner, q, kind, peer):
        return pltpu.make_async_remote_copy(
            src_ref=source, dst_ref=at(owner, q), send_sem=send_sem.at[kind, q], recv_sem=recv_sem.at[kind, q],
            device_id={"row": peer}, device_id_type=MESH,
        )

    def own(q, kind):
        return copy(x_ref.at[pl.ds(q * size, size), :], me, q, kind, (by_x, by_y)[kind])

    half = parts // 2
    order = list(range(parts))
    for a, b in zip(order, order[half:] + order[:half]):
        own(a, 0).start()
        own(b, 1).start()
    keep = pltpu.make_async_copy(x_ref, out_ref.at[pl.ds(pl.multiple_of(me * rows, rows), rows), :], own_sem)
    keep.start()

    def arrival(owner, q, kind):
        return copy(at(owner, q), owner, q, kind, (by_x, by_y)[kind % 2])

    def onward(q):
        if q < half:
            return copy(at(by_x, q), by_x, q, 2, by_y)
        return copy(at(by_y, q), by_y, q, 2, by_x)

    for q in range(half):
        arrival(by_x, q, 0).wait_recv()
        onward(q).start()
        arrival(by_y, q + half, 1).wait_recv()
        onward(q + half).start()
    keep.wait()
    for q in range(parts):
        if q >= half:
            arrival(by_x, q, 0).wait_recv()
        else:
            arrival(by_y, q, 1).wait_recv()
        arrival(corner, q, 2).wait_recv()
        own(q, 0).wait_send()
        own(q, 1).wait_send()
        onward(q).wait_send()


def gather_rows(x, n, parts=8):
    square = n == 4
    shape = (3, parts) if square else (n,)
    return pl.pallas_call(
        functools.partial(gather_square_kernel, parts) if square else functools.partial(gather_kernel, n),
        in_specs=[pl.BlockSpec(memory_space=pl.ANY)],
        out_specs=pl.BlockSpec(memory_space=pl.ANY),
        out_shape=jax.ShapeDtypeStruct((n * x.shape[0], x.shape[1]), F32),
        scratch_shapes=[
            pltpu.SemaphoreType.DMA(shape),
            pltpu.SemaphoreType.DMA(shape),
            pltpu.SemaphoreType.DMA,
        ],
        compiler_params=params(0),
    )(x)


def middle_kernel(
    zs, chunks, skew, extra, hop,
    part_ref, weight_ref, cot_ref,
    out_ref, grads_ref, term_ref,
    acc, mate, from_left, from_right, grad, inner, w_hi, w_lo, t_hi, t_lo,
    own_sem, mate_send, mate_recv, right_send, right_recv, left_send, left_recv,
    on_send, back_send, line_recv, share_send, share_recv, keep_sem,
):
    col = lax.axis_index("col")
    z, k = lax.div(col, 2), lax.rem(col, 2)
    rows = cot_ref.shape[0]
    size = rows // chunks
    pair = {"col": z * 2 + (1 - k)}
    right, left = {"col": jnp.minimum(z + 1, zs - 1) * 2 + k}, {"col": jnp.maximum(z - 1, 0) * 2 + k}
    has_left, has_right = z > 0, z < zs - 1

    barrier = pltpu.get_barrier_semaphore()
    pl.semaphore_signal(barrier, inc=1, device_id=pair, device_id_type=MESH)

    @pl.when(has_left)
    def _():
        pl.semaphore_signal(barrier, inc=1, device_id=left, device_id_type=MESH)

    @pl.when(has_right)
    def _():
        pl.semaphore_signal(barrier, inc=1, device_id=right, device_id_type=MESH)

    pl.semaphore_wait(barrier, 1 + has_left.astype(jnp.int32) + has_right.astype(jnp.int32))

    def span(c):
        return pl.ds(pl.multiple_of(c * size, size), size)

    def place(owner, core, c):
        return pl.ds(pl.multiple_of((owner * 2 + core) * rows + c * size, size), size)

    def remote(src, dst, send, recv, device):
        return pltpu.make_async_remote_copy(
            src_ref=src, dst_ref=dst, send_sem=send, recv_sem=recv, device_id=device, device_id_type=MESH
        )

    def own_copy(d):
        block = part_ref.at[pl.ds(pl.multiple_of((d * 2 + k) * rows, rows), rows), :]
        return pltpu.make_async_copy(block, acc.at[d], own_sem.at[d])

    def mate_copy(d, c):
        return remote(
            part_ref.at[place(d, 1 - k, c), :], mate.at[d, span(c)], mate_send.at[d, c], mate_recv.at[d, c], pair
        )

    def to_right(d, c):
        return remote(acc.at[d, span(c)], from_left.at[d, span(c)], right_send.at[d, c], right_recv.at[d, c], right)

    def to_left(d, c):
        return remote(acc.at[d, span(c)], from_right.at[d, span(c)], left_send.at[d, c], left_recv.at[d, c], left)

    def own_on(c):
        return remote(grad.at[span(c)], grads_ref.at[place(z, k, c), :], on_send.at[z, c], line_recv.at[z, c], right)

    def own_back(c):
        return remote(grad.at[span(c)], grads_ref.at[place(z, k, c), :], back_send.at[c], line_recv.at[z, c], left)

    def own_share(c):
        return remote(grad.at[span(c)], grads_ref.at[place(z, k, c), :], share_send.at[z, c], share_recv.at[z, c], pair)

    def own_keep(c):
        return pltpu.make_async_copy(grad.at[span(c)], grads_ref.at[place(z, k, c), :], keep_sem.at[c])

    def pass_on(s, c, device):
        where = grads_ref.at[place(s, k, c), :]
        return remote(where, where, on_send.at[s, c], line_recv.at[s, c], device)

    def share(s, core, c):
        where = grads_ref.at[place(s, core, c), :]
        return remote(where, where, share_send.at[s, c], share_recv.at[s, c], pair)

    @pl.loop(0, zs)
    def _(d):
        own_copy(d).start()

    @pl.loop(0, chunks)
    def _(c):
        @pl.loop(0, zs)
        def _(d):
            mate_copy(d, c).start()

    @pl.loop(0, zs)
    def _(d):
        own_copy(d).wait()

    def add_mate(d, c):
        mate_copy(d, c).wait_recv()
        acc[d, span(c)] += mate[d, span(c)]

    def reduce_right(c):
        @pl.loop(0, zs - 1 - z)
        def _(i):
            far = zs - 1 - i
            add_mate(far, c)

            @pl.when(has_left)
            def _():
                to_right(far, c).wait_recv()
                acc[far, span(c)] += from_left[far, span(c)]

            to_right(far, c).start()

    def reduce_left(c):
        @pl.loop(0, z)
        def _(i):
            add_mate(i, c)

            @pl.when(has_right)
            def _():
                to_left(i, c).wait_recv()
                acc[i, span(c)] += from_right[i, span(c)]

            to_left(i, c).start()

    def finish_chunk(c):
        add_mate(z, c)

        @pl.when(has_left)
        def _():
            to_right(z, c).wait_recv()
            acc[z, span(c)] += from_left[z, span(c)]

        @pl.when(has_right)
        def _():
            to_left(z, c).wait_recv()
            acc[z, span(c)] += from_right[z, span(c)]

        if DENSE:
            summed = acc[z, span(c)]
            pre = dot3(summed, w_hi[...], w_lo[...])
            sigma = jax.nn.sigmoid(pre)
            out_ref[span(c), :] = pre * sigma
            grad_pre = cot_ref[span(c), :] * sigma * (1.0 + pre * (1.0 - sigma))
            inner[span(c), :] = grad_pre
            grad[span(c)] = dot3(grad_pre, t_hi[...], t_lo[...])

        @pl.when(has_right)
        def _():
            own_on(c).start()

        @pl.when(has_left)
        def _():
            own_back(c).start()

        own_share(c).start()
        own_keep(c).start()

    def relay(source, c, has_next, device):
        pass_on(source, c, device).wait_recv()

        @pl.when(has_next)
        def _():
            pass_on(source, c, device).start()

        share(source, k, c).start()

    w_hi[...], w_lo[...] = split(weight_ref[...])
    t_hi[...], t_lo[...] = split(weight_ref[...].T)

    def sent(owner):
        return skew * jnp.maximum(owner, zs - 1 - owner) + extra

    def at_step(c, act):
        @pl.when((c >= 0) & (c < chunks))
        def _():
            act(c)

    @pl.loop(0, chunks + (skew + hop) * (zs - 1) + extra)
    def _(s):
        at_step(s - skew * z, reduce_right)
        at_step(s - skew * (zs - 1 - z), reduce_left)
        at_step(s - sent(z), finish_chunk)

        @pl.loop(1, zs)
        def _(i):
            low, high = z - i, z + i

            @pl.when(low >= 0)
            def _():
                at_step(s - sent(low) - hop * i, lambda c: relay(low, c, has_right, right))

            @pl.when(high < zs)
            def _():
                at_step(s - sent(high) - hop * i, lambda c: relay(high, c, has_left, left))

    term_ref[...] = lax.dot_general(
        acc[z], inner[...], (((0,), (0,)), ((), ())), precision=HIGHEST, preferred_element_type=F32
    )

    @pl.loop(0, chunks)
    def _(c):
        own_share(c).wait_send()
        own_keep(c).wait()

        @pl.when(has_right)
        def _():
            own_on(c).wait_send()

        @pl.when(has_left)
        def _():
            own_back(c).wait_send()

        @pl.loop(0, zs)
        def _(d):
            mate_copy(d, c).wait_send()
            share(d, 1 - k, c).wait_recv()

            @pl.when(d > z)
            def _():
                to_right(d, c).wait_send()
                share(d, k, c).wait_send()

                @pl.when(has_left)
                def _():
                    pass_on(d, c, left).wait_send()

            @pl.when(d < z)
            def _():
                to_left(d, c).wait_send()
                share(d, k, c).wait_send()

                @pl.when(has_right)
                def _():
                    pass_on(d, c, right).wait_send()


def middle(part, weight, cotangent, n_col, chunks=8, skew=1, extra=0, hop=1):
    rows, width = cotangent.shape
    zs = n_col // 2
    grid2 = pltpu.SemaphoreType.DMA((zs, chunks))
    vmem = pl.BlockSpec(memory_space=pltpu.VMEM)
    blocks, own = pltpu.VMEM((zs, rows, width), F32), pltpu.VMEM((rows, width), F32)
    half = pltpu.VMEM((width, width), BF16)
    return pl.pallas_call(
        functools.partial(middle_kernel, zs, chunks, skew, extra, hop),
        in_specs=[pl.BlockSpec(memory_space=pl.ANY), vmem, vmem],
        out_specs=(vmem, pl.BlockSpec(memory_space=pl.ANY), vmem),
        out_shape=(
            jax.ShapeDtypeStruct((rows, width), F32),
            jax.ShapeDtypeStruct((n_col * rows, width), F32),
            jax.ShapeDtypeStruct((width, width), F32),
        ),
        scratch_shapes=[
            blocks, blocks, blocks, blocks, own, own, half, half, half, half,
            pltpu.SemaphoreType.DMA((zs,)), grid2, grid2, grid2, grid2, grid2, grid2,
            grid2, pltpu.SemaphoreType.DMA((chunks,)), grid2, grid2, grid2, pltpu.SemaphoreType.DMA((chunks,)),
        ],
        compiler_params=params(1),
    )(part, weight, cotangent)


def last_kernel(
    n_row, n_col, scale,
    part_ref, term_ref,
    out_ref, total_ref,
    arrived, first, second,
    own_sem, send_sem, recv_sem, send1, recv1, send2, recv2, send3, recv3,
):
    row, col = lax.axis_index("row"), lax.axis_index("col")
    rows = out_ref.shape[0]
    piece = term_ref.shape[0] // n_col
    barrier = pltpu.get_barrier_semaphore()
    for j in range(1, n_row):
        pl.semaphore_signal(barrier, inc=1, device_id={"row": lax.rem(row + j, n_row)}, device_id_type=MESH)
    for j in range(1, n_col):
        pl.semaphore_signal(barrier, inc=1, device_id={"col": lax.rem(col + j, n_col)}, device_id_type=MESH)
    pl.semaphore_wait(barrier, n_row + n_col - 2)

    def block(i):
        return part_ref.at[pl.ds(pl.multiple_of(i * rows, rows), rows), :]

    def rows_of(i):
        return pl.ds(pl.multiple_of(i * piece, piece), piece)

    def bulk(j):
        to = lax.rem(row + j, n_row)
        return pltpu.make_async_remote_copy(
            src_ref=block(to), dst_ref=arrived.at[j], send_sem=send_sem.at[j], recv_sem=recv_sem.at[j],
            device_id={"row": to}, device_id_type=MESH,
        )

    def scatter(j):
        to = lax.rem(col + j, n_col)
        return pltpu.make_async_remote_copy(
            src_ref=term_ref.at[rows_of(to), :], dst_ref=first.at[j], send_sem=send1.at[j], recv_sem=recv1.at[j],
            device_id={"col": to}, device_id_type=MESH,
        )

    def exchange(j, slot):
        return pltpu.make_async_remote_copy(
            src_ref=first.at[0], dst_ref=second.at[slot], send_sem=send2.at[j], recv_sem=recv2.at[j],
            device_id={"row": lax.rem(row + j, n_row)}, device_id_type=MESH,
        )

    def spread(j, owner):
        where = total_ref.at[rows_of(owner), :]
        return pltpu.make_async_remote_copy(
            src_ref=where, dst_ref=where, send_sem=send3.at[j], recv_sem=recv3.at[j],
            device_id={"col": lax.rem(col + j, n_col)}, device_id_type=MESH,
        )

    own = pltpu.make_async_copy(block(row), arrived.at[0], own_sem)
    own.start()
    for j in range(1, n_col):
        scatter(j).start()
    bulk(1).start()
    first[0] = term_ref[rows_of(col), :]
    for j in range(1, n_col):
        scatter(j).wait_recv()
        first[0] += first[j]
    for j in range(1, n_row):
        exchange(j, row).start()
    for j in range(2, n_row):
        bulk(j).start()
    second[row] = first[0]
    for j in range(1, n_row):
        exchange(j, lax.rem(row + n_row - j, n_row)).wait_recv()
    summed = second[0]
    for i in range(1, n_row):
        summed += second[i]
    total_ref[rows_of(col), :] = summed * scale
    for j in range(1, n_col):
        spread(j, col).start()
    own.wait()
    for j in range(1, n_row):
        bulk(j).wait_recv()
    out_ref[...] = arrived[0]
    for j in range(1, n_row):
        out_ref[...] += arrived[j]
    for j in range(1, n_row):
        bulk(j).wait_send()
        exchange(j, row).wait_send()
    for j in range(1, n_col):
        scatter(j).wait_send()
        spread(j, col).wait_send()
        spread(j, lax.rem(col + n_col - j, n_col)).wait_recv()


def last_square_kernel(
    parts, n_col, scale,
    part_ref, term_ref,
    out_ref, total_ref,
    mine, middle_rows, near, through, final, first, second,
    own_sem, middle_sem, send_sem, recv_sem, send1, recv1, send2, recv2, send3, recv3,
):
    row, col = lax.axis_index("row"), lax.axis_index("col")
    rows = out_ref.shape[0]
    size, half = rows // parts, parts // 2
    piece = term_ref.shape[0] // n_col
    x_bit, y_bit = lax.rem(row, 2), lax.div(row, 2)
    by_x, by_y, corner = y_bit * 2 + (1 - x_bit), (1 - y_bit) * 2 + x_bit, 3 - row
    barrier = pltpu.get_barrier_semaphore()
    for peer in (by_x, by_y, corner):
        pl.semaphore_signal(barrier, inc=1, device_id={"row": peer}, device_id_type=MESH)
    for j in range(1, n_col):
        pl.semaphore_signal(barrier, inc=1, device_id={"col": lax.rem(col + j, n_col)}, device_id_type=MESH)
    pl.semaphore_wait(barrier, n_col + 2)

    def remote(src, dst, send, recv, device):
        return pltpu.make_async_remote_copy(
            src_ref=src, dst_ref=dst, send_sem=send, recv_sem=recv, device_id=device, device_id_type=MESH
        )

    def span(q):
        return pl.ds(q * size, size)

    def block(owner, q):
        return part_ref.at[pl.ds(pl.multiple_of(owner * rows + q * size, size), size), :]

    def rows_of(i):
        return pl.ds(pl.multiple_of(i * piece, piece), piece)

    def hop(q, second_hop):
        return {"row": by_x if (q < half) != second_hop else by_y}

    def far(q):
        return remote(block(corner, q), through.at[span(q), :], send_sem.at[0, q], recv_sem.at[0, q], hop(q, False))

    def direct(q):
        to = by_x if q < half else by_y
        return remote(block(to, q), near.at[span(q), :], send_sem.at[1, q], recv_sem.at[1, q], hop(q, False))

    def onward(q):
        return remote(
            middle_rows.at[span(q), :], final.at[span(q), :], send_sem.at[2, q], recv_sem.at[2, q], hop(q, True)
        )

    def load_middle(q):
        return pltpu.make_async_copy(block(by_y if q < half else by_x, q), middle_rows.at[span(q), :], middle_sem.at[q])

    def scatter(j):
        to = lax.rem(col + j, n_col)
        return remote(term_ref.at[rows_of(to), :], first.at[j], send1.at[j], recv1.at[j], {"col": to})

    def exchange(j, slot):
        return remote(first.at[0], second.at[slot], send2.at[j], recv2.at[j], {"row": lax.rem(row + j, 4)})

    def spread(j, owner):
        where = total_ref.at[rows_of(owner), :]
        return remote(where, where, send3.at[j], recv3.at[j], {"col": lax.rem(col + j, n_col)})

    order = [q for pair in zip(range(half), range(half, parts)) for q in pair]
    for j in range(1, n_col):
        scatter(j).start()
    for q in order:
        far(q).start()
    own = pltpu.make_async_copy(part_ref.at[pl.ds(pl.multiple_of(row * rows, rows), rows), :], mine, own_sem)
    own.start()
    for q in order:
        load_middle(q).start()
    first[0] = term_ref[rows_of(col), :]
    for j in range(1, n_col):
        scatter(j).wait_recv()
        first[0] += first[j]
    for j in range(1, 4):
        exchange(j, row).start()
    for q in order:
        direct(q).start()
    second[row] = first[0]
    for q in order:
        load_middle(q).wait()
        far(q).wait_recv()
        middle_rows[span(q), :] += through[span(q), :]
        onward(q).start()
    for j in range(1, 4):
        exchange(j, lax.rem(row + 4 - j, 4)).wait_recv()
    total_ref[rows_of(col), :] = (second[0] + second[1] + second[2] + second[3]) * scale
    for j in range(1, n_col):
        spread(j, col).start()
    own.wait()
    for q in order:
        direct(q).wait_recv()
        onward(q).wait_recv()
        out_ref[span(q), :] = mine[span(q), :] + near[span(q), :] + final[span(q), :]
    for q in order:
        far(q).wait_send()
        direct(q).wait_send()
        onward(q).wait_send()
    for j in range(1, 4):
        exchange(j, row).wait_send()
    for j in range(1, n_col):
        scatter(j).wait_send()
        spread(j, col).wait_send()
        spread(j, lax.rem(col + n_col - j, n_col)).wait_recv()


def last_square(part, term, n_col, scale, parts):
    rows, width = part.shape[0] // 4, part.shape[1]
    piece = term.shape[0] // n_col
    vmem, own = pl.BlockSpec(memory_space=pltpu.VMEM), pltpu.VMEM((rows, width), F32)
    bulk, by_row, by_col = (pltpu.SemaphoreType.DMA(n) for n in ((3, parts), (4,), (n_col,)))
    return pl.pallas_call(
        functools.partial(last_square_kernel, parts, n_col, scale),
        in_specs=[pl.BlockSpec(memory_space=pl.ANY), vmem],
        out_specs=(vmem, vmem),
        out_shape=(jax.ShapeDtypeStruct((rows, width), F32), jax.ShapeDtypeStruct(term.shape, F32)),
        scratch_shapes=[
            own, own, own, own, own,
            pltpu.VMEM((n_col, piece, width), F32),
            pltpu.VMEM((4, piece, width), F32),
            pltpu.SemaphoreType.DMA, pltpu.SemaphoreType.DMA((parts,)), bulk, bulk,
            by_col, by_col, by_row, by_row, by_col, by_col,
        ],
        compiler_params=params(2),
    )(part, term)


def last(part, term, n_row, n_col, scale, parts=4):
    if n_row == 4:
        return last_square(part, term, n_col, scale, parts)
    rows, width = part.shape[0] // n_row, part.shape[1]
    piece = term.shape[0] // n_col
    vmem = pl.BlockSpec(memory_space=pltpu.VMEM)
    by_row, by_col = pltpu.SemaphoreType.DMA((n_row,)), pltpu.SemaphoreType.DMA((n_col,))
    return pl.pallas_call(
        functools.partial(last_kernel, n_row, n_col, scale),
        in_specs=[pl.BlockSpec(memory_space=pl.ANY), vmem],
        out_specs=(vmem, vmem),
        out_shape=(jax.ShapeDtypeStruct((rows, width), F32), jax.ShapeDtypeStruct(term.shape, F32)),
        scratch_shapes=[
            pltpu.VMEM((n_row, rows, width), F32),
            pltpu.VMEM((n_col, piece, width), F32),
            pltpu.VMEM((n_row, piece, width), F32),
            pltpu.SemaphoreType.DMA, by_row, by_row, by_col, by_col, by_row, by_row, by_col, by_col,
        ],
        compiler_params=params(2),
    )(part, term)


def local(n_row, n_col, features, weight, cotangent, tile_values, tile_rows, tile_cols, tile_count):
    tiles, row_ids, col_ids = tile_values[0, 0], tile_rows[0, 0], tile_cols[0, 0]
    count = tile_count.reshape(1)
    rows = features.shape[0]
    gathered = gather_rows(features, n_row)
    part = combine_tiles(tiles, col_ids, row_ids, count, gathered, rows * n_col, False)
    output, grads, term = middle(part, weight, cotangent, n_col)
    part_grad = combine_tiles(tiles, row_ids, col_ids, count, grads, rows * n_row, True)
    scale = 1.0 / math.sqrt(rows * n_row * n_col)
    returned, weight_grad = last(part_grad, term, n_row, n_col, scale)
    return (output, returned, weight_grad)


def solution(mesh):
    placed = (
        P(("col", "row"), None),
        P(),
        P(("row", "col"), None),
        P("row", "col", None, None, None),
        P("row", "col", None),
        P("row", "col", None),
        P("row", "col"),
    )
    return jax.shard_map(
        functools.partial(local, mesh.shape["row"], mesh.shape["col"]),
        mesh=mesh,
        in_specs=placed,
        out_specs=(P(("row", "col"), None), P(("col", "row"), None), P()),
        check_vma=False,
    )
```

```python
import functools
import math

import jax
import jax.numpy as jnp
from jax import lax
from jax.experimental import pallas as pl
from jax.experimental.pallas import tpu as pltpu
from jax.sharding import PartitionSpec as P

F32 = jnp.float32
BF16 = jnp.bfloat16
MESH = pl.DeviceIdType.MESH
VMEM_LIMIT = 60 * 1024 * 1024
HIGHEST = lax.Precision.HIGHEST


def split(x):
    hi = x.astype(BF16)
    return hi, (x - hi.astype(F32)).astype(BF16)


def dot3(a, b_hi, b_lo):
    a_hi, a_lo = split(a)
    dot = functools.partial(jnp.dot, preferred_element_type=F32)
    return dot(a_hi, b_hi) + (dot(a_lo, b_hi) + dot(a_hi, b_lo))


def params(collective_id=None):
    if collective_id is None:
        return pltpu.CompilerParams(vmem_limit_bytes=VMEM_LIMIT)
    return pltpu.CompilerParams(
        vmem_limit_bytes=VMEM_LIMIT, collective_id=collective_id, has_side_effects=True
    )


def tile_kernel(group, transpose, fetch_ref, put_ref, count_ref, tiles_ref, source_ref, *refs):
    *carry, out_ref, hi_ref, lo_ref = refs
    step = pl.program_id(0)
    edge = tiles_ref.shape[1]

    @pl.when(step == 0)
    def _():
        out_ref[...] = jnp.zeros_like(out_ref)
        if carry:
            carry[1][...] = carry[0][...]

        @pl.loop(0, source_ref.shape[0] // edge)
        def _(b):
            rows = pl.ds(pl.multiple_of(b * edge, edge), edge)
            hi, lo = split(source_ref[rows, :])
            hi_ref[rows, :] = hi
            lo_ref[rows, :] = lo

    @pl.when(step * group < count_ref[0])
    def _():
        for t in range(group):
            slot = step * group + t
            fetch = pl.ds(pl.multiple_of(fetch_ref[slot] * edge, edge), edge)
            put = pl.ds(pl.multiple_of(put_ref[slot] * edge, edge), edge)
            tile = tiles_ref[t]
            if transpose:
                tile = tile.T
            a_hi, a_lo = split(tile)
            b_hi, b_lo = hi_ref[fetch, :], lo_ref[fetch, :]
            product = jnp.dot(
                jnp.concatenate([a_hi, a_lo], axis=1),
                jnp.concatenate([b_hi, b_hi], axis=0),
                preferred_element_type=F32,
            ) + jnp.dot(a_hi, b_lo, preferred_element_type=F32)
            out_ref[put, :] += product


def combine_tiles(tiles, fetch_ids, put_ids, count, source, out_rows, transpose, carry=()):
    slots, edge, _ = tiles.shape
    width = source.shape[1]
    group = math.gcd(16, slots)

    def tile_index(i, fetch, put, n):
        return (jnp.minimum(i, (n[0] - 1) // group), 0, 0)

    def whole(shape):
        return pl.BlockSpec(shape, lambda i, *_: (0, 0), pipeline_mode=pl.Buffered(1))

    return pl.pallas_call(
        functools.partial(tile_kernel, group, transpose),
        grid_spec=pltpu.PrefetchScalarGridSpec(
            num_scalar_prefetch=3,
            grid=(slots // group,),
            in_specs=[
                pl.BlockSpec((group, edge, edge), tile_index),
                whole(source.shape),
                *(whole(x.shape) for x in carry),
            ],
            out_specs=(*(whole(x.shape) for x in carry), whole((out_rows, width))),
            scratch_shapes=[pltpu.VMEM(source.shape, BF16), pltpu.VMEM(source.shape, BF16)],
        ),
        out_shape=(
            *(jax.ShapeDtypeStruct(x.shape, F32) for x in carry),
            jax.ShapeDtypeStruct((out_rows, width), F32),
        ),
        compiler_params=params(),
    )(fetch_ids, put_ids, count, tiles, source, *carry)


def gather_kernel(n, x_ref, out_ref, send_sem, recv_sem, own_sem):
    me = lax.axis_index("row")
    rows = x_ref.shape[0]
    barrier = pltpu.get_barrier_semaphore()
    for j in range(1, n):
        pl.semaphore_signal(barrier, inc=1, device_id={"row": lax.rem(me + j, n)}, device_id_type=MESH)
    pl.semaphore_wait(barrier, n - 1)

    def copy(j, block):
        return pltpu.make_async_remote_copy(
            src_ref=x_ref,
            dst_ref=out_ref.at[pl.ds(pl.multiple_of(block * rows, rows), rows), :],
            send_sem=send_sem.at[j],
            recv_sem=recv_sem.at[j],
            device_id={"row": lax.rem(me + j, n)},
            device_id_type=MESH,
        )

    for j in range(1, n):
        copy(j, me).start()
    own = pltpu.make_async_copy(x_ref, out_ref.at[pl.ds(pl.multiple_of(me * rows, rows), rows), :], own_sem)
    own.start()
    own.wait()
    for j in range(1, n):
        copy(j, me).wait_send()
        copy(j, lax.rem(me + n - j, n)).wait_recv()


def gather_square_kernel(parts, x_ref, out_ref, send_sem, recv_sem, own_sem):
    me = lax.axis_index("row")
    rows = x_ref.shape[0]
    size = rows // parts
    x_bit, y_bit = lax.rem(me, 2), lax.div(me, 2)
    by_x, by_y = y_bit * 2 + (1 - x_bit), (1 - y_bit) * 2 + x_bit
    corner = 3 - me
    barrier = pltpu.get_barrier_semaphore()
    for peer in (by_x, by_y):
        pl.semaphore_signal(barrier, inc=1, device_id={"row": peer}, device_id_type=MESH)
    pl.semaphore_wait(barrier, 2)

    def at(owner, q):
        return out_ref.at[pl.ds(pl.multiple_of(owner * rows + q * size, size), size), :]

    def copy(source, owner, q, kind, peer):
        return pltpu.make_async_remote_copy(
            src_ref=source, dst_ref=at(owner, q), send_sem=send_sem.at[kind, q], recv_sem=recv_sem.at[kind, q],
            device_id={"row": peer}, device_id_type=MESH,
        )

    def own(q, kind):
        return copy(x_ref.at[pl.ds(q * size, size), :], me, q, kind, (by_x, by_y)[kind])

    half = parts // 2
    order = list(range(parts))
    for a, b in zip(order, order[half:] + order[:half]):
        own(a, 0).start()
        own(b, 1).start()
    keep = pltpu.make_async_copy(x_ref, out_ref.at[pl.ds(pl.multiple_of(me * rows, rows), rows), :], own_sem)
    keep.start()

    def arrival(owner, q, kind):
        return copy(at(owner, q), owner, q, kind, (by_x, by_y)[kind % 2])

    def onward(q):
        if q < half:
            return copy(at(by_x, q), by_x, q, 2, by_y)
        return copy(at(by_y, q), by_y, q, 2, by_x)

    for q in range(half):
        arrival(by_x, q, 0).wait_recv()
        onward(q).start()
        arrival(by_y, q + half, 1).wait_recv()
        onward(q + half).start()
    keep.wait()
    for q in range(parts):
        if q >= half:
            arrival(by_x, q, 0).wait_recv()
        else:
            arrival(by_y, q, 1).wait_recv()
        arrival(corner, q, 2).wait_recv()
        own(q, 0).wait_send()
        own(q, 1).wait_send()
        onward(q).wait_send()


def gather_rows(x, n, parts=4):
    square = n == 4
    shape = (3, parts) if square else (n,)
    return pl.pallas_call(
        functools.partial(gather_square_kernel, parts) if square else functools.partial(gather_kernel, n),
        in_specs=[pl.BlockSpec(memory_space=pl.ANY)],
        out_specs=pl.BlockSpec(memory_space=pl.ANY),
        out_shape=jax.ShapeDtypeStruct((n * x.shape[0], x.shape[1]), F32),
        scratch_shapes=[
            pltpu.SemaphoreType.DMA(shape),
            pltpu.SemaphoreType.DMA(shape),
            pltpu.SemaphoreType.DMA,
        ],
        compiler_params=params(0),
    )(x)


def middle_kernel(
    zs, chunks, skew, extra, hop,
    part_ref, weight_ref, cot_ref,
    out_ref, grads_ref, term_ref,
    acc, mate, from_left, from_right, grad, inner, w_hi, w_lo, t_hi, t_lo,
    own_sem, mate_send, mate_recv, right_send, right_recv, left_send, left_recv,
    on_send, back_send, line_recv, share_send, share_recv, keep_sem,
):
    col = lax.axis_index("col")
    z, k = lax.div(col, 2), lax.rem(col, 2)
    rows = cot_ref.shape[0]
    size = rows // chunks
    pair = {"col": z * 2 + (1 - k)}
    right, left = {"col": jnp.minimum(z + 1, zs - 1) * 2 + k}, {"col": jnp.maximum(z - 1, 0) * 2 + k}
    has_left, has_right = z > 0, z < zs - 1

    barrier = pltpu.get_barrier_semaphore()
    pl.semaphore_signal(barrier, inc=1, device_id=pair, device_id_type=MESH)

    @pl.when(has_left)
    def _():
        pl.semaphore_signal(barrier, inc=1, device_id=left, device_id_type=MESH)

    @pl.when(has_right)
    def _():
        pl.semaphore_signal(barrier, inc=1, device_id=right, device_id_type=MESH)

    pl.semaphore_wait(barrier, 1 + has_left.astype(jnp.int32) + has_right.astype(jnp.int32))

    def span(c):
        return pl.ds(pl.multiple_of(c * size, size), size)

    def place(owner, core, c):
        return pl.ds(pl.multiple_of((owner * 2 + core) * rows + c * size, size), size)

    def remote(src, dst, send, recv, device):
        return pltpu.make_async_remote_copy(
            src_ref=src, dst_ref=dst, send_sem=send, recv_sem=recv, device_id=device, device_id_type=MESH
        )

    def own_copy(d):
        block = part_ref.at[pl.ds(pl.multiple_of((d * 2 + k) * rows, rows), rows), :]
        return pltpu.make_async_copy(block, acc.at[d], own_sem.at[d])

    def mate_copy(d, c):
        return remote(
            part_ref.at[place(d, 1 - k, c), :], mate.at[d, span(c)], mate_send.at[d, c], mate_recv.at[d, c], pair
        )

    def to_right(d, c):
        return remote(acc.at[d, span(c)], from_left.at[d, span(c)], right_send.at[d, c], right_recv.at[d, c], right)

    def to_left(d, c):
        return remote(acc.at[d, span(c)], from_right.at[d, span(c)], left_send.at[d, c], left_recv.at[d, c], left)

    def own_on(c):
        return remote(grad.at[span(c)], grads_ref.at[place(z, k, c), :], on_send.at[z, c], line_recv.at[z, c], right)

    def own_back(c):
        return remote(grad.at[span(c)], grads_ref.at[place(z, k, c), :], back_send.at[c], line_recv.at[z, c], left)

    def own_share(c):
        return remote(grad.at[span(c)], grads_ref.at[place(z, k, c), :], share_send.at[z, c], share_recv.at[z, c], pair)

    def own_keep(c):
        return pltpu.make_async_copy(grad.at[span(c)], grads_ref.at[place(z, k, c), :], keep_sem.at[c])

    def pass_on(s, c, device):
        where = grads_ref.at[place(s, k, c), :]
        return remote(where, where, on_send.at[s, c], line_recv.at[s, c], device)

    def share(s, core, c):
        where = grads_ref.at[place(s, core, c), :]
        return remote(where, where, share_send.at[s, c], share_recv.at[s, c], pair)

    @pl.loop(0, zs)
    def _(d):
        own_copy(d).start()

    @pl.loop(0, chunks)
    def _(c):
        @pl.loop(0, zs)
        def _(d):
            mate_copy(d, c).start()

    @pl.loop(0, zs)
    def _(d):
        own_copy(d).wait()

    def add_mate(d, c):
        mate_copy(d, c).wait_recv()
        acc[d, span(c)] += mate[d, span(c)]

    def reduce_right(c):
        @pl.loop(0, zs - 1 - z)
        def _(i):
            far = zs - 1 - i
            add_mate(far, c)

            @pl.when(has_left)
            def _():
                to_right(far, c).wait_recv()
                acc[far, span(c)] += from_left[far, span(c)]

            to_right(far, c).start()

    def reduce_left(c):
        @pl.loop(0, z)
        def _(i):
            add_mate(i, c)

            @pl.when(has_right)
            def _():
                to_left(i, c).wait_recv()
                acc[i, span(c)] += from_right[i, span(c)]

            to_left(i, c).start()

    def finish_chunk(c):
        add_mate(z, c)

        @pl.when(has_left)
        def _():
            to_right(z, c).wait_recv()
            acc[z, span(c)] += from_left[z, span(c)]

        @pl.when(has_right)
        def _():
            to_left(z, c).wait_recv()
            acc[z, span(c)] += from_right[z, span(c)]

        if True:
            summed = acc[z, span(c)]
            pre = dot3(summed, w_hi[...], w_lo[...])
            sigma = jax.nn.sigmoid(pre)
            out_ref[span(c), :] = pre * sigma
            grad_pre = cot_ref[span(c), :] * sigma * (1.0 + pre * (1.0 - sigma))
            inner[span(c), :] = grad_pre
            grad[span(c)] = dot3(grad_pre, t_hi[...], t_lo[...])

        @pl.when(has_right)
        def _():
            own_on(c).start()

        @pl.when(has_left)
        def _():
            own_back(c).start()

        own_share(c).start()
        own_keep(c).start()

    def relay(source, c, has_next, device):
        pass_on(source, c, device).wait_recv()

        @pl.when(has_next)
        def _():
            pass_on(source, c, device).start()

        share(source, k, c).start()

    w_hi[...], w_lo[...] = split(weight_ref[...])
    t_hi[...], t_lo[...] = split(weight_ref[...].T)

    def sent(owner):
        return skew * jnp.maximum(owner, zs - 1 - owner) + extra

    def at_step(c, act):
        @pl.when((c >= 0) & (c < chunks))
        def _():
            act(c)

    @pl.loop(0, chunks + (skew + hop) * (zs - 1) + extra)
    def _(s):
        at_step(s - skew * z, reduce_right)
        at_step(s - skew * (zs - 1 - z), reduce_left)
        at_step(s - sent(z), finish_chunk)

        @pl.loop(1, zs)
        def _(i):
            low, high = z - i, z + i

            @pl.when(low >= 0)
            def _():
                at_step(s - sent(low) - hop * i, lambda c: relay(low, c, has_right, right))

            @pl.when(high < zs)
            def _():
                at_step(s - sent(high) - hop * i, lambda c: relay(high, c, has_left, left))

    term_ref[...] = lax.dot_general(
        acc[z], inner[...], (((0,), (0,)), ((), ())), precision=HIGHEST, preferred_element_type=F32
    )

    @pl.loop(0, chunks)
    def _(c):
        own_share(c).wait_send()
        own_keep(c).wait()

        @pl.when(has_right)
        def _():
            own_on(c).wait_send()

        @pl.when(has_left)
        def _():
            own_back(c).wait_send()

        @pl.loop(0, zs)
        def _(d):
            mate_copy(d, c).wait_send()
            share(d, 1 - k, c).wait_recv()

            @pl.when(d > z)
            def _():
                to_right(d, c).wait_send()
                share(d, k, c).wait_send()

                @pl.when(has_left)
                def _():
                    pass_on(d, c, left).wait_send()

            @pl.when(d < z)
            def _():
                to_left(d, c).wait_send()
                share(d, k, c).wait_send()

                @pl.when(has_right)
                def _():
                    pass_on(d, c, right).wait_send()


def middle(part, weight, cotangent, n_col, chunks=8, skew=1, extra=0, hop=1):
    rows, width = cotangent.shape
    zs = n_col // 2
    grid2 = pltpu.SemaphoreType.DMA((zs, chunks))
    vmem = pl.BlockSpec(memory_space=pltpu.VMEM)
    blocks, own = pltpu.VMEM((zs, rows, width), F32), pltpu.VMEM((rows, width), F32)
    half = pltpu.VMEM((width, width), BF16)
    return pl.pallas_call(
        functools.partial(middle_kernel, zs, chunks, skew, extra, hop),
        in_specs=[pl.BlockSpec(memory_space=pl.ANY), vmem, vmem],
        out_specs=(vmem, pl.BlockSpec(memory_space=pl.ANY), vmem),
        out_shape=(
            jax.ShapeDtypeStruct((rows, width), F32),
            jax.ShapeDtypeStruct((n_col * rows, width), F32),
            jax.ShapeDtypeStruct((width, width), F32),
        ),
        scratch_shapes=[
            blocks, blocks, blocks, blocks, own, own, half, half, half, half,
            pltpu.SemaphoreType.DMA((zs,)), grid2, grid2, grid2, grid2, grid2, grid2,
            grid2, pltpu.SemaphoreType.DMA((chunks,)), grid2, grid2, grid2, pltpu.SemaphoreType.DMA((chunks,)),
        ],
        compiler_params=params(1),
    )(part, weight, cotangent)


def last_kernel(
    n_row, n_col, scale,
    part_ref, term_ref,
    out_ref, total_ref,
    arrived, first, second,
    own_sem, send_sem, recv_sem, send1, recv1, send2, recv2, send3, recv3,
):
    row, col = lax.axis_index("row"), lax.axis_index("col")
    rows = out_ref.shape[0]
    piece = term_ref.shape[0] // n_col
    barrier = pltpu.get_barrier_semaphore()
    for j in range(1, n_row):
        pl.semaphore_signal(barrier, inc=1, device_id={"row": lax.rem(row + j, n_row)}, device_id_type=MESH)
    for j in range(1, n_col):
        pl.semaphore_signal(barrier, inc=1, device_id={"col": lax.rem(col + j, n_col)}, device_id_type=MESH)
    pl.semaphore_wait(barrier, n_row + n_col - 2)

    def block(i):
        return part_ref.at[pl.ds(pl.multiple_of(i * rows, rows), rows), :]

    def rows_of(i):
        return pl.ds(pl.multiple_of(i * piece, piece), piece)

    def bulk(j):
        to = lax.rem(row + j, n_row)
        return pltpu.make_async_remote_copy(
            src_ref=block(to), dst_ref=arrived.at[j], send_sem=send_sem.at[j], recv_sem=recv_sem.at[j],
            device_id={"row": to}, device_id_type=MESH,
        )

    def scatter(j):
        to = lax.rem(col + j, n_col)
        return pltpu.make_async_remote_copy(
            src_ref=term_ref.at[rows_of(to), :], dst_ref=first.at[j], send_sem=send1.at[j], recv_sem=recv1.at[j],
            device_id={"col": to}, device_id_type=MESH,
        )

    def exchange(j, slot):
        return pltpu.make_async_remote_copy(
            src_ref=first.at[0], dst_ref=second.at[slot], send_sem=send2.at[j], recv_sem=recv2.at[j],
            device_id={"row": lax.rem(row + j, n_row)}, device_id_type=MESH,
        )

    def spread(j, owner):
        where = total_ref.at[rows_of(owner), :]
        return pltpu.make_async_remote_copy(
            src_ref=where, dst_ref=where, send_sem=send3.at[j], recv_sem=recv3.at[j],
            device_id={"col": lax.rem(col + j, n_col)}, device_id_type=MESH,
        )

    own = pltpu.make_async_copy(block(row), arrived.at[0], own_sem)
    own.start()
    for j in range(1, n_col):
        scatter(j).start()
    bulk(1).start()
    first[0] = term_ref[rows_of(col), :]
    for j in range(1, n_col):
        scatter(j).wait_recv()
        first[0] += first[j]
    for j in range(1, n_row):
        exchange(j, row).start()
    for j in range(2, n_row):
        bulk(j).start()
    second[row] = first[0]
    for j in range(1, n_row):
        exchange(j, lax.rem(row + n_row - j, n_row)).wait_recv()
    summed = second[0]
    for i in range(1, n_row):
        summed += second[i]
    total_ref[rows_of(col), :] = summed * scale
    for j in range(1, n_col):
        spread(j, col).start()
    own.wait()
    for j in range(1, n_row):
        bulk(j).wait_recv()
    out_ref[...] = arrived[0]
    for j in range(1, n_row):
        out_ref[...] += arrived[j]
    for j in range(1, n_row):
        bulk(j).wait_send()
        exchange(j, row).wait_send()
    for j in range(1, n_col):
        scatter(j).wait_send()
        spread(j, col).wait_send()
        spread(j, lax.rem(col + n_col - j, n_col)).wait_recv()


def last_square_kernel(
    parts, n_col, scale,
    part_ref, term_ref,
    out_ref, total_ref,
    mine, middle_rows, near, through, final, first, second,
    own_sem, middle_sem, send_sem, recv_sem, send1, recv1, send2, recv2, send3, recv3,
):
    row, col = lax.axis_index("row"), lax.axis_index("col")
    rows = out_ref.shape[0]
    size, half = rows // parts, parts // 2
    piece = term_ref.shape[0] // n_col
    x_bit, y_bit = lax.rem(row, 2), lax.div(row, 2)
    by_x, by_y, corner = y_bit * 2 + (1 - x_bit), (1 - y_bit) * 2 + x_bit, 3 - row
    barrier = pltpu.get_barrier_semaphore()
    for peer in (by_x, by_y, corner):
        pl.semaphore_signal(barrier, inc=1, device_id={"row": peer}, device_id_type=MESH)
    for j in range(1, n_col):
        pl.semaphore_signal(barrier, inc=1, device_id={"col": lax.rem(col + j, n_col)}, device_id_type=MESH)
    pl.semaphore_wait(barrier, n_col + 2)

    def remote(src, dst, send, recv, device):
        return pltpu.make_async_remote_copy(
            src_ref=src, dst_ref=dst, send_sem=send, recv_sem=recv, device_id=device, device_id_type=MESH
        )

    def span(q):
        return pl.ds(q * size, size)

    def block(owner, q):
        return part_ref.at[pl.ds(pl.multiple_of(owner * rows + q * size, size), size), :]

    def rows_of(i):
        return pl.ds(pl.multiple_of(i * piece, piece), piece)

    def hop(q, second_hop):
        return {"row": by_x if (q < half) != second_hop else by_y}

    def far(q):
        return remote(block(corner, q), through.at[span(q), :], send_sem.at[0, q], recv_sem.at[0, q], hop(q, False))

    def direct(q):
        to = by_x if q < half else by_y
        return remote(block(to, q), near.at[span(q), :], send_sem.at[1, q], recv_sem.at[1, q], hop(q, False))

    def onward(q):
        return remote(
            middle_rows.at[span(q), :], final.at[span(q), :], send_sem.at[2, q], recv_sem.at[2, q], hop(q, True)
        )

    def load_middle(q):
        return pltpu.make_async_copy(block(by_y if q < half else by_x, q), middle_rows.at[span(q), :], middle_sem.at[q])

    def scatter(j):
        to = lax.rem(col + j, n_col)
        return remote(term_ref.at[rows_of(to), :], first.at[j], send1.at[j], recv1.at[j], {"col": to})

    def exchange(j, slot):
        return remote(first.at[0], second.at[slot], send2.at[j], recv2.at[j], {"row": lax.rem(row + j, 4)})

    def spread(j, owner):
        where = total_ref.at[rows_of(owner), :]
        return remote(where, where, send3.at[j], recv3.at[j], {"col": lax.rem(col + j, n_col)})

    order = [q for pair in zip(range(half), range(half, parts)) for q in pair]
    for j in range(1, n_col):
        scatter(j).start()
    for q in order:
        far(q).start()
    own = pltpu.make_async_copy(part_ref.at[pl.ds(pl.multiple_of(row * rows, rows), rows), :], mine, own_sem)
    own.start()
    for q in order:
        load_middle(q).start()
    for q in order:
        direct(q).start()
    first[0] = term_ref[rows_of(col), :]
    for j in range(1, n_col):
        scatter(j).wait_recv()
        first[0] += first[j]
    for j in range(1, 4):
        exchange(j, row).start()
    second[row] = first[0]
    for q in order:
        load_middle(q).wait()
        far(q).wait_recv()
        middle_rows[span(q), :] += through[span(q), :]
        onward(q).start()
    for j in range(1, 4):
        exchange(j, lax.rem(row + 4 - j, 4)).wait_recv()
    total_ref[rows_of(col), :] = (second[0] + second[1] + second[2] + second[3]) * scale
    for j in range(1, n_col):
        spread(j, col).start()
    own.wait()
    for q in order:
        direct(q).wait_recv()
        onward(q).wait_recv()
        out_ref[span(q), :] = mine[span(q), :] + near[span(q), :] + final[span(q), :]
    for q in order:
        far(q).wait_send()
        direct(q).wait_send()
        onward(q).wait_send()
    for j in range(1, 4):
        exchange(j, row).wait_send()
    for j in range(1, n_col):
        scatter(j).wait_send()
        spread(j, col).wait_send()
        spread(j, lax.rem(col + n_col - j, n_col)).wait_recv()


def last_square(part, term, n_col, scale, parts):
    rows, width = part.shape[0] // 4, part.shape[1]
    piece = term.shape[0] // n_col
    vmem, own = pl.BlockSpec(memory_space=pltpu.VMEM), pltpu.VMEM((rows, width), F32)
    bulk, by_row, by_col = (pltpu.SemaphoreType.DMA(n) for n in ((3, parts), (4,), (n_col,)))
    return pl.pallas_call(
        functools.partial(last_square_kernel, parts, n_col, scale),
        in_specs=[pl.BlockSpec(memory_space=pl.ANY), vmem],
        out_specs=(vmem, vmem),
        out_shape=(jax.ShapeDtypeStruct((rows, width), F32), jax.ShapeDtypeStruct(term.shape, F32)),
        scratch_shapes=[
            own, own, own, own, own,
            pltpu.VMEM((n_col, piece, width), F32),
            pltpu.VMEM((4, piece, width), F32),
            pltpu.SemaphoreType.DMA, pltpu.SemaphoreType.DMA((parts,)), bulk, bulk,
            by_col, by_col, by_row, by_row, by_col, by_col,
        ],
        compiler_params=params(2),
    )(part, term)


def last(part, term, n_row, n_col, scale, parts=4):
    if n_row == 4:
        return last_square(part, term, n_col, scale, parts)
    rows, width = part.shape[0] // n_row, part.shape[1]
    piece = term.shape[0] // n_col
    vmem = pl.BlockSpec(memory_space=pltpu.VMEM)
    by_row, by_col = pltpu.SemaphoreType.DMA((n_row,)), pltpu.SemaphoreType.DMA((n_col,))
    return pl.pallas_call(
        functools.partial(last_kernel, n_row, n_col, scale),
        in_specs=[pl.BlockSpec(memory_space=pl.ANY), vmem],
        out_specs=(vmem, vmem),
        out_shape=(jax.ShapeDtypeStruct((rows, width), F32), jax.ShapeDtypeStruct(term.shape, F32)),
        scratch_shapes=[
            pltpu.VMEM((n_row, rows, width), F32),
            pltpu.VMEM((n_col, piece, width), F32),
            pltpu.VMEM((n_row, piece, width), F32),
            pltpu.SemaphoreType.DMA, by_row, by_row, by_col, by_col, by_row, by_row, by_col, by_col,
        ],
        compiler_params=params(2),
    )(part, term)


def local(n_row, n_col, features, weight, cotangent, tile_values, tile_rows, tile_cols, tile_count):
    tiles, row_ids, col_ids = tile_values[0, 0], tile_rows[0, 0], tile_cols[0, 0]
    count = tile_count.reshape(1)
    rows = features.shape[0]
    gathered = gather_rows(features, n_row)
    (part,) = combine_tiles(tiles, col_ids, row_ids, count, gathered, rows * n_col, False)
    output, grads, term = middle(part, weight, cotangent, n_col)
    output, part_grad = combine_tiles(tiles, row_ids, col_ids, count, grads, rows * n_row, True, (output,))
    scale = 1.0 / math.sqrt(rows * n_row * n_col)
    returned, weight_grad = last(part_grad, term, n_row, n_col, scale)
    return (output, returned, weight_grad)


def solution(mesh):
    placed = (
        P(("col", "row"), None),
        P(),
        P(("row", "col"), None),
        P("row", "col", None, None, None),
        P("row", "col", None),
        P("row", "col", None),
        P("row", "col"),
    )
    return jax.shard_map(
        functools.partial(local, mesh.shape["row"], mesh.shape["col"]),
        mesh=mesh,
        in_specs=placed,
        out_specs=(P(("row", "col"), None), P(("col", "row"), None), P()),
        check_vma=False,
    )
```
